32 devices in a mesh: seq: 8 (over z, core), fsdp: 4 (over y, x).
Axes of the slice: x: 2, y: 2, z: 4, core: 2. Of those that a mesh axis runs over, the one named last changes fastest.
Arguments:
- queries: bfloat16 [4, 2048, 4096], P('fsdp', 'seq'), may hold values from -60 to 60
- keys: bfloat16 [4, 2048, 4096], P('fsdp', 'seq'), may hold values from -4.8 to 4.8
- values: bfloat16 [4, 2048, 4096], P('fsdp', 'seq'), may hold values from -6 to 6
- out_weight: bfloat16 [4096, 3072], P(('seq', 'fsdp')), may hold values from -0.75 to 0.75
- block_lists: int32 [4, 32, 16, 8], P('fsdp'), may hold values from 0 to 15, as said below
- block_counts: int32 [4, 32, 16], P('fsdp'), may hold values from 1 to 8, as said below
Outputs:
- projected: bfloat16 [4, 2048, 3072], P('fsdp', 'seq')
The draws below stay inside these ranges and needn't reach their ends.
Inputs may be any that keep to these rules, and one draw needn't show every extreme that they name: `block_lists`: entry j = 0 of every list is the query block itself; the 8 entries of a list are distinct blocks; entries at slots j >= block_counts are ignored. `block_counts`: in every sequence some head and query block has 8 live slots.
All inputs are finite; a program needn't handle non-finite values.
Results may differ from the reference program's by a relative error of at most 0.0085.
Values may be sent and summed in bfloat16 or wider, within the bound.
No kernel may reach another device: no remote copies, remote signals or barrier semaphores. Data moves between devices by JAX's collectives and lax.ppermute only.
A program may use at most 128 MiB of HBM per device.

```python
import jax
import jax.numpy as jnp
from jax import lax

HEADS = 32
HDIM = 128
DOUT = 3072
BLOCK = 128
KMAX = 8
SEQS = 4
LEN = 2048
QB = 16


def paired_fields(key):
    base_key = jax.random.fold_in(key, 11)
    first_key, second_key = jax.random.split(base_key)
    extent = (SEQS, LEN, HEADS * HDIM)
    key_field = jnp.clip(1.2 * jax.random.normal(first_key, extent, jnp.float32), -4.75, 4.75)
    query_field = jnp.clip(1.2 * jax.random.normal(second_key, extent, jnp.float32), -4.75, 4.75)
    return (query_field, key_field)


def draw_queries(key, part):
    return paired_fields(key)[0].astype(jnp.bfloat16)


def draw_keys(key, part):
    return paired_fields(key)[1].astype(jnp.bfloat16)


def shuffle_one(subkey):
    return jax.random.permutation(subkey, QB - 1).astype(jnp.int32)


def draw_block_lists(key, part):
    base_key = jax.random.fold_in(key, 23)
    row_total = SEQS * HEADS * QB
    subkeys = jax.random.split(base_key, row_total)
    orders = jax.vmap(shuffle_one)(subkeys)
    own_block = (jnp.arange(row_total, dtype=jnp.int32) % QB)[:, None]
    others = (own_block + 1 + orders[:, :KMAX - 1]) % QB
    listed = jnp.concatenate([own_block, others], axis=1)
    return listed.reshape(SEQS, HEADS, QB, KMAX).astype(jnp.int32)


def draw_block_counts(key, part):
    base_key = jax.random.fold_in(key, 37)
    cap_key, raw_key, head_key, block_key = jax.random.split(base_key, 4)
    ceilings = jax.random.randint(cap_key, (SEQS, HEADS, 1), 2, KMAX + 1, dtype=jnp.int32)
    raw_draw = jax.random.randint(raw_key, (SEQS, HEADS, QB), 0, 1 << 20, dtype=jnp.int32)
    counted = 1 + raw_draw % ceilings
    chosen_head = jax.random.randint(head_key, (SEQS, 1, 1), 0, HEADS, dtype=jnp.int32)
    chosen_block = jax.random.randint(block_key, (SEQS, 1, 1), 0, QB, dtype=jnp.int32)
    head_ids = lax.broadcasted_iota(jnp.int32, (SEQS, HEADS, QB), 1)
    block_ids = lax.broadcasted_iota(jnp.int32, (SEQS, HEADS, QB), 2)
    peak_spot = (head_ids == chosen_head) & (block_ids == chosen_block)
    return jnp.where(peak_spot, KMAX, counted).astype(jnp.int32)


def shard_levels(own_key, shape, cuts, smallest, high):
    factor_of = 1.0
    for axis_at, blocks in cuts:
        draws = jax.random.uniform(jax.random.fold_in(jax.random.fold_in(own_key, 6), axis_at), (blocks,), jnp.float32, smallest / len(cuts), high / len(cuts))
        factor_of = factor_of * jnp.repeat(jnp.exp(draws), shape[axis_at] // blocks).reshape((-1,) + (1,) * (len(shape) - 1 - axis_at))
    return factor_of


def gaussian(key, shape, width, reach, cuts=(), kind=jnp.bfloat16):
    entries = jax.random.normal(key, shape, jnp.float32) * width
    if len(cuts) > 0:
        entries = shard_levels(key, shape, cuts, -0.22, 0.18) * entries
    return jnp.clip(entries, min=-reach, max=reach).astype(kind)


def setup_inputs(seed: int = 0) -> dict:
    streams_of = jax.random.split(jax.random.key(seed), 7)
    queries = draw_queries(jax.random.fold_in(streams_of[6], 71), 0)
    keys = draw_keys(jax.random.fold_in(streams_of[6], 71), 0)
    values = gaussian(streams_of[2], (SEQS, LEN, HEADS * HDIM), 1.0, 6.0, ((0, 4), (1, 8)))
    out_weight = gaussian(streams_of[3], (HEADS * HDIM, DOUT), (HEADS * HDIM // 64) ** -0.5, 0.75, ((0, 32),))
    block_lists = draw_block_lists(jax.random.fold_in(streams_of[6], 71), 0)
    block_counts = draw_block_counts(jax.random.fold_in(streams_of[6], 71), 0)
    return dict(queries=queries, keys=keys, values=values, out_weight=out_weight, block_lists=block_lists, block_counts=block_counts)


def attend_one(operands):
    query_rows, key_rows, value_rows, block_ids, live_counts = operands
    query_blocks = query_rows.reshape(QB, BLOCK, HDIM).astype(jnp.float32)
    key_tiles = key_rows.reshape(QB, BLOCK, HDIM)[block_ids].reshape(QB, KMAX * BLOCK, HDIM).astype(jnp.float32)
    value_tiles = value_rows.reshape(QB, BLOCK, HDIM)[block_ids].reshape(QB, KMAX * BLOCK, HDIM).astype(jnp.float32)
    scores = jnp.einsum('qpd,qkd->qpk', query_blocks, key_tiles) * (HDIM ** -0.5)
    usable = jnp.arange(KMAX, dtype=jnp.int32)[None, :] < live_counts[:, None]
    usable = jnp.repeat(usable, BLOCK, axis=1)[:, None, :]
    scores = jnp.where(usable, scores, -jnp.inf)
    weights = jnp.exp(scores - jnp.max(scores, axis=2, keepdims=True))
    totals = jnp.sum(weights, axis=2, keepdims=True)
    rounded = lax.optimization_barrier(weights.astype(jnp.bfloat16)).astype(jnp.float32)
    mixed = jnp.einsum('qpk,qkd->qpd', rounded, value_tiles) / totals
    return mixed.astype(jnp.bfloat16).reshape(LEN, HDIM)


def split_heads(field):
    return field.reshape(SEQS, LEN, HEADS, HDIM).transpose(0, 2, 1, 3).reshape(SEQS * HEADS, LEN, HDIM)


def reference(queries, keys, values, out_weight, block_lists, block_counts):
    attended = lax.map(attend_one, (split_heads(queries), split_heads(keys), split_heads(values),
                                    block_lists.reshape(SEQS * HEADS, QB, KMAX),
                                    block_counts.reshape(SEQS * HEADS, QB)))
    attended = attended.reshape(SEQS, HEADS, LEN, HDIM).transpose(0, 2, 1, 3).reshape(SEQS * LEN, HEADS * HDIM)
    projected = jnp.dot(attended, out_weight, preferred_element_type=jnp.float32).astype(jnp.bfloat16)
    return projected.reshape(SEQS, LEN, DOUT)
```

```python
import functools
import math

import jax
import jax.numpy as jnp
from jax import lax
from jax.experimental import pallas as pl
from jax.experimental.pallas import tpu as pltpu
from jax.sharding import PartitionSpec as P

BLOCK = 128


def attend_kernel(base, width, slots, lists_ref, counts_ref, qkv_ref, out_ref):
    sources, tokens, lanes = qkv_ref.shape
    heads = lanes // (3 * width)
    per = tokens // BLOCK
    blocks = sources * per
    scale = width ** (-0.5) * math.log2(math.e)

    def rows_of(block):
        return block // per, pl.ds(pl.multiple_of((block % per) * BLOCK, BLOCK), BLOCK)

    for member in range(heads):
        q_cols = slice(member * width, (member + 1) * width)
        k_cols = slice((heads + member) * width, (heads + member + 1) * width)
        v_cols = slice((2 * heads + member) * width, (2 * heads + member + 1) * width)

        def one(i, carry, member=member, q_cols=q_cols, k_cols=k_cols, v_cols=v_cols):
            live = counts_ref[base + member, i]
            src, rows = rows_of(i)

            def branch(pairs):
                picked = [rows_of(lists_ref[base + member, i * slots + j]) for j in range(2 * pairs)]
                q = qkv_ref[src, rows, q_cols]
                scores = []
                for n in range(pairs):
                    k = jnp.concatenate([qkv_ref[s, r, k_cols] for s, r in picked[2 * n : 2 * n + 2]], axis=0)
                    scores.append(lax.dot_general(q, k, (((1,), (1,)), ((), ())), preferred_element_type=jnp.float32))
                second = lax.broadcasted_iota(jnp.int32, scores[-1].shape, 1) < BLOCK * (live - 2 * (pairs - 1))
                scores[-1] = jnp.where(second, scores[-1], -jnp.inf)
                top = functools.reduce(jnp.maximum, scores)
                top = jnp.max(top, axis=1, keepdims=True) * scale
                total = None
                mixed = None
                for n in range(pairs):
                    weights = jnp.exp2(scores[n] * scale - top)
                    v = jnp.concatenate([qkv_ref[s, r, v_cols] for s, r in picked[2 * n : 2 * n + 2]], axis=0)
                    part = jnp.dot(weights.astype(jnp.bfloat16), v, preferred_element_type=jnp.float32)
                    total = weights if total is None else total + weights
                    mixed = part if mixed is None else mixed + part
                totals = jnp.sum(total, axis=1, keepdims=True)
                out_ref[src, rows, q_cols] = (mixed / totals).astype(out_ref.dtype)

            for pairs in range(1, slots // 2 + 1):
                pl.when((live + 1) // 2 == pairs)(functools.partial(branch, pairs))
            return carry

        lax.fori_loop(0, blocks, one, 0)


def attend(qkv, lists, counts, base, width):
    sources, tokens, lanes = qkv.shape
    slots = lists.shape[1] // counts.shape[1]
    smem = pl.BlockSpec(memory_space=pltpu.SMEM)
    vmem = pl.BlockSpec(memory_space=pltpu.VMEM)
    flops = 4 * (sources * tokens) * (slots * BLOCK // 2) * (lanes // 3)
    return pl.pallas_call(
        functools.partial(attend_kernel, base, width, slots),
        out_shape=jax.ShapeDtypeStruct((sources, tokens, lanes // 3), jnp.bfloat16),
        in_specs=[smem, smem, vmem],
        out_specs=vmem,
        compiler_params=pltpu.CompilerParams(vmem_limit_bytes=32 * 1024 * 1024),
        cost_estimate=pl.CostEstimate(flops=flops, bytes_accessed=qkv.size * 2, transcendentals=flops // 512),
    )(lists, counts, qkv)


def shards(queries, keys, values, out_weight, block_lists, block_counts):
    groups = lax.axis_size("seq")
    rank = lax.axis_index("seq")
    head_count = block_counts.shape[1]
    blocks = block_counts.shape[2]
    width = queries.shape[2] // head_count
    here = head_count // groups
    tokens = queries.shape[1]
    lists = lax.dynamic_slice_in_dim(block_lists[0], rank * here, here).reshape(here, -1)
    counts = lax.dynamic_slice_in_dim(block_counts[0], rank * here, here)

    fields = [x[0].reshape(tokens, groups, here, width) for x in (queries, keys, values)]
    weights = lax.all_gather(out_weight, ("fsdp", "seq"), axis=0, tiled=True)
    rows = out_weight.shape[0]
    per_head = width // rows

    result = None
    for member in range(here):
        mine = jnp.concatenate([f[:, :, member].transpose(1, 0, 2) for f in fields], axis=2)
        qkv = lax.all_to_all(mine, "seq", split_axis=0, concat_axis=0, tiled=True)
        out = attend(qkv, lists, counts, member, width)
        back = lax.all_to_all(out, "seq", split_axis=0, concat_axis=0, tiled=True)
        back = back.reshape(groups, tokens, per_head, rows).transpose(1, 2, 0, 3).reshape(tokens, groups * width)
        part = jnp.dot(
            back,
            weights[member * groups * width : (member + 1) * groups * width],
            preferred_element_type=jnp.float32,
        )
        result = part if result is None else result + part
    return result.astype(jnp.bfloat16)[None]


def solution(mesh):
    return jax.shard_map(
        shards,
        mesh=mesh,
        in_specs=(
            P("fsdp", "seq", None),
            P("fsdp", "seq", None),
            P("fsdp", "seq", None),
            P(("seq", "fsdp"), None),
            P("fsdp", None, None, None),
            P("fsdp", None, None),
        ),
        out_specs=P("fsdp", "seq", None),
        check_vma=False,
    )
```

```python
import functools
import math

import jax
import jax.numpy as jnp
from jax import lax
from jax.experimental import pallas as pl
from jax.experimental.pallas import tpu as pltpu
from jax.sharding import PartitionSpec as P

BLOCK = 128
VMEM = pl.BlockSpec(memory_space=pltpu.VMEM)
SMEM = pl.BlockSpec(memory_space=pltpu.SMEM)
ANY = pl.BlockSpec(memory_space=pl.ANY)
HBM = pl.BlockSpec(memory_space=pltpu.HBM)


def limit(mib):
    return pltpu.CompilerParams(vmem_limit_bytes=mib * 1024 * 1024)


def layout_kernel(members, here, width, *refs):
    fields, sem = refs[:3], refs[-1]
    out_refs = refs[-1 - len(members) : -1]
    groups = out_refs[0].shape[0]
    copies = []
    for m, member in enumerate(members):
        for g in range(groups):
            start = (g * here + member) * width
            for n, field in enumerate(fields):
                copies.append(
                    pltpu.make_async_copy(
                        field.at[:, pl.ds(start, width)],
                        out_refs[m].at[g, :, pl.ds(n * width, width)],
                        sem.at[m, g, n],
                    )
                )
    for copy in copies:
        copy.start()
    for copy in copies:
        copy.wait()


def lay_out(fields, members, groups, here, width, extra):
    tokens = fields[0].shape[0]
    count = len(members)
    return pl.pallas_call(
        functools.partial(layout_kernel, members, here, width),
        out_shape=[jax.ShapeDtypeStruct((groups, tokens, 3 * width), jnp.bfloat16)] * count,
        in_specs=[HBM] * 3 + [ANY] * len(extra),
        out_specs=[HBM] * count,
        scratch_shapes=[pltpu.SemaphoreType.DMA((count, groups, 3))],
        compiler_params=limit(16),
        cost_estimate=pl.CostEstimate(flops=1, bytes_accessed=1, transcendentals=0),
    )(*fields, *extra)


def attend_kernel(member, width, slots, rank_ref, lists_ref, counts_ref, *refs):
    qkv_ref, out_refs, held = refs[0], refs[1:-1], refs[-1]
    sources, tokens, _ = qkv_ref.shape
    per = tokens // BLOCK
    scale = width ** (-0.5) * math.log2(math.e)
    q_cols, k_cols, v_cols = (slice(n * width, (n + 1) * width) for n in range(3))

    def rows_of(block):
        return block // per, pl.ds(pl.multiple_of((block % per) * BLOCK, BLOCK), BLOCK)

    def one(at, carry):
        part = at // per
        rows = pl.ds(pl.multiple_of((at % per) * BLOCK, BLOCK), BLOCK)
        src = part ^ rank_ref[0]
        i = src * per + at % per
        live = counts_ref[member, i]

        def branch(pairs):
            picked = [rows_of(lists_ref[member, i * slots + j]) for j in range(2 * pairs)]
            q = qkv_ref[src, rows, q_cols]
            scores = []
            for n in range(pairs):
                k = jnp.concatenate([qkv_ref[s, r, k_cols] for s, r in picked[2 * n : 2 * n + 2]], axis=0)
                scores.append(lax.dot_general(q, k, (((1,), (1,)), ((), ())), preferred_element_type=jnp.float32))
            usable = lax.broadcasted_iota(jnp.int32, scores[-1].shape, 1) < BLOCK * (live - 2 * (pairs - 1))
            scores[-1] = jnp.where(usable, scores[-1], -jnp.inf)
            top = functools.reduce(jnp.maximum, scores)
            top = jnp.max(top, axis=1, keepdims=True) * scale
            total = None
            mixed = None
            for n in range(pairs):
                weights = jnp.exp2(scores[n] * scale - top)
                v = jnp.concatenate([qkv_ref[s, r, v_cols] for s, r in picked[2 * n : 2 * n + 2]], axis=0)
                product = jnp.dot(weights.astype(jnp.bfloat16), v, preferred_element_type=jnp.float32)
                total = weights if total is None else total + weights
                mixed = product if mixed is None else mixed + product
            totals = jnp.sum(total, axis=1, keepdims=True)
            held[part, rows, :] = (mixed / totals).astype(held.dtype)

        for pairs in range(1, slots // 2 + 1):
            pl.when((live + 1) // 2 == pairs)(functools.partial(branch, pairs))
        return carry

    lax.fori_loop(0, sources * per, one, 0)
    each = sources // len(out_refs)
    for n, out_ref in enumerate(out_refs):
        for m in range(each):
            out_ref[m * tokens : (m + 1) * tokens, :] = held[n * each + m]


def attend(qkv, rank, lists, counts, member, width, each):
    sources, tokens, _ = qkv.shape
    slots = lists.shape[1] // counts.shape[1]
    return pl.pallas_call(
        functools.partial(attend_kernel, member, width, slots),
        out_shape=[jax.ShapeDtypeStruct((each * tokens, width), jnp.bfloat16)] * (sources // each),
        in_specs=[SMEM, SMEM, SMEM, VMEM],
        out_specs=[VMEM] * (sources // each),
        scratch_shapes=[pltpu.VMEM((sources, tokens, width), jnp.bfloat16)],
        compiler_params=limit(32),
        cost_estimate=pl.CostEstimate(flops=1, bytes_accessed=1, transcendentals=0),
    )(rank, lists, counts, qkv)


def project_kernel(terms, n_rows, n_blocks, n_before, *refs):
    rows, blocks = refs[:n_rows], refs[n_rows : n_rows + n_blocks]
    before = refs[n_rows + n_blocks : n_rows + n_blocks + n_before]
    out_refs = refs[n_rows + n_blocks + n_before : -3]
    held, total, sem = refs[-3:]
    slots = held.shape[0]
    copies = [
        pltpu.make_async_copy(blocks[block].at[member], held.at[n % slots], sem.at[n % slots])
        for n, (block, member, _) in enumerate(terms)
    ]
    for copy in copies[:slots]:
        copy.start()
    wide = total.shape[-1]
    step = wide // 4
    for n, (_, _, picked) in enumerate(terms):
        copies[n].wait()
        left = jnp.concatenate([rows[r][...] for r in picked], axis=1)
        for at in range(0, wide, step):
            cols = slice(at, at + step)
            part = jnp.dot(left, held[n % slots, :, cols], preferred_element_type=jnp.float32)
            if n:
                part = part + total[:, cols]
            else:
                for other in before:
                    part = part + other[:, cols]
            if n < len(terms) - 1:
                total[:, cols] = part
            else:
                tall = part.shape[0] // len(out_refs)
                for m, out_ref in enumerate(out_refs):
                    out_ref[:, cols] = part[m * tall : (m + 1) * tall].astype(out_ref.dtype)
        if n + slots < len(terms):
            copies[n + slots].start()


def project(rows, blocks, terms, before, dtypes):
    tall = rows[0].shape[0]
    depth, wide = blocks[0].shape[1:]
    slots, outs = min(4, len(terms)), len(dtypes)
    return pl.pallas_call(
        functools.partial(project_kernel, terms, len(rows), len(blocks), len(before)),
        out_shape=[jax.ShapeDtypeStruct((tall // outs, wide), dtype) for dtype in dtypes],
        in_specs=[VMEM] * len(rows) + [ANY] * len(blocks) + [VMEM] * len(before),
        out_specs=[VMEM] * outs,
        scratch_shapes=[
            pltpu.VMEM((slots, depth, wide), jnp.bfloat16),
            pltpu.VMEM((tall, wide), jnp.float32),
            pltpu.SemaphoreType.DMA((slots,)),
        ],
        compiler_params=limit(48),
        cost_estimate=pl.CostEstimate(flops=1, bytes_accessed=1, transcendentals=0),
    )(*rows, *blocks, *before)


def along_z(pairs):
    return [(2 * i + c, 2 * j + c) for i, j in pairs for c in (0, 1)]


def after(value, *others):
    return lax.optimization_barrier((value, *others))[0]


def xor(p, groups):
    return [(i, i ^ p) for i in range(groups)]


UP = [(0, 1), (1, 2), (2, 3)]
DOWN = [(j, i) for i, j in UP]


def exchange(x):
    return lax.all_to_all(x, "seq", split_axis=0, concat_axis=0, tiled=True)


def shards_lines(fields, weight, rank, lists, counts, here, width):
    groups = 8
    chip = lax.axis_index("seq") // 2
    number = jnp.full((1,), rank, jnp.int32)
    swap = xor(1, groups)

    def send(value, pairs, *holds):
        return lax.ppermute(after(value, *holds) if holds else value, "seq", pairs)

    def send_back(out):
        unit = groups // len(out)
        return [out[0]] + [send(out[p], xor(p * unit, groups)) for p in range(1, len(out))]

    def attend_member(qkv, member, each):
        return attend(qkv, number, lists, counts, member, width, each)

    up = send(weight, along_z(UP))
    down = send(weight, along_z(DOWN))
    x0, x1, x2, x3 = lay_out(fields, (0, 1, 2, 3), groups, here, width, [])
    near = jnp.concatenate([weight, jnp.where(chip % 2 == 0, down, up)], axis=0)
    near, x0, x1, x2, x3 = lax.optimization_barrier((near, x0, x1, x2, x3))
    first = lax.all_gather(near, "fsdp", axis=0, tiled=False)
    qkv0 = exchange(x0)
    up2 = send(up, along_z(UP[1:]), near)
    down2 = send(down, along_z(DOWN[:2]), near)
    up2, down2, qkv0 = lax.optimization_barrier((up2, down2, qkv0))
    qkv1 = exchange(after(x1, up2))
    out0 = attend_member(qkv0, 0, 2)
    up3 = send(up2, along_z(UP[2:]), *out0)
    down3 = send(down2, along_z(DOWN[:1]), *out0)
    back0 = send_back(out0)
    up3, down3, qkv1 = lax.optimization_barrier((up3, down3, qkv1))
    inner = (chip == 1) | (chip == 2)
    low = chip < 2
    opposite = jnp.where(inner, jnp.where(low, down, up), jnp.where(low, down3, up3))
    far = jnp.concatenate([jnp.where(low, down2, up2), opposite], axis=0)
    second = lax.all_gather(far, "fsdp", axis=0, tiled=False)
    qkv2 = exchange(after(x2, qkv1, far))
    out1 = attend_member(qkv1, 1, 2)
    back1 = send_back(out1)
    qkv2, *back0 = lax.optimization_barrier((qkv2, *back0))
    qkv3 = exchange(after(x3, qkv2, first, *out1))
    out2 = attend_member(qkv2, 2, 2)
    qkv3, *rest = lax.optimization_barrier((qkv3, *back1, *out2))
    back1, out2 = rest[:4], rest[4:]
    back2 = send_back(out2)
    out3 = attend_member(qkv3, 3, 2)
    back0, back1, back2, out3 = lax.optimization_barrier((back0, back1, back2, out3))
    back3 = send_back(out3)
    blocks = [first, second]

    def terms(member, at):
        return [(h, member, (4 * at + 2 * h, 4 * at + 2 * h + 1)) for h in (0, 1)]

    (both,) = project(back0 + back1 + back2, blocks, terms(0, 0) + terms(1, 1) + terms(2, 2), [], (jnp.float32,))
    mine, theirs = project(back3, blocks, terms(3, 0), [both], (jnp.float32, jnp.bfloat16))
    return (mine + send(theirs, swap).astype(jnp.float32)).astype(jnp.bfloat16)


def shards_any(fields, weight, rank, lists, counts, here, width, groups):
    number = jnp.full((1,), rank, jnp.int32)
    rows = weight.shape[0]
    gathered = lax.all_gather(weight, ("fsdp", "seq"), axis=0, tiled=True)
    gathered = gathered.reshape(here, width // rows, groups, rows, -1).transpose(0, 2, 1, 3, 4)
    gathered = gathered.reshape(here, groups, width, -1)
    ready = lay_out(fields, tuple(range(here)), groups, here, width, [])
    result = None
    for member in range(here):
        out = attend(exchange(ready[member]), number, lists, counts, member, width, 1)
        for p in range(groups):
            part = jnp.dot(
                lax.ppermute(out[p], "seq", xor(p, groups)) if p else out[0],
                lax.dynamic_index_in_dim(gathered[member], rank ^ p, 0, keepdims=False),
                preferred_element_type=jnp.float32,
            )
            result = part if result is None else result + part
    return result.astype(jnp.bfloat16)


def shards(queries, keys, values, out_weight, block_lists, block_counts):
    groups = lax.axis_size("seq")
    rank = lax.axis_index("seq")
    head_count = block_counts.shape[1]
    width = queries.shape[2] // head_count
    here = head_count // groups
    lists = lax.dynamic_slice_in_dim(block_lists[0], rank * here, here).reshape(here, -1)
    counts = lax.dynamic_slice_in_dim(block_counts[0], rank * here, here)
    fields = [x[0] for x in (queries, keys, values)]
    if groups == 8 and here == 4 and lax.axis_size("fsdp") == 4 and out_weight.shape[0] == width:
        result = shards_lines(fields, out_weight, rank, lists, counts, here, width)
    else:
        result = shards_any(fields, out_weight, rank, lists, counts, here, width, groups)
    return result[None]


def solution(mesh):
    return jax.shard_map(
        shards,
        mesh=mesh,
        in_specs=(
            P("fsdp", "seq", None),
            P("fsdp", "seq", None),
            P("fsdp", "seq", None),
            P(("seq", "fsdp"), None),
            P("fsdp", None, None, None),
            P("fsdp", None, None),
        ),
        out_specs=P("fsdp", "seq", None),
        check_vma=False,
    )
```

```python
import functools
import math

import jax
import jax.numpy as jnp
from jax import lax
from jax.experimental import pallas as pl
from jax.experimental.pallas import tpu as pltpu
from jax.sharding import PartitionSpec as P

BLOCK = 128
VMEM = pl.BlockSpec(memory_space=pltpu.VMEM)
SMEM = pl.BlockSpec(memory_space=pltpu.SMEM)
ANY = pl.BlockSpec(memory_space=pl.ANY)
FREE = pl.CostEstimate(flops=1, bytes_accessed=1, transcendentals=0)


def limit(mib):
    return pltpu.CompilerParams(vmem_limit_bytes=mib * 1024 * 1024)


def layout_kernel(steps, here, width, place_ref, *refs):
    fields, sem = refs[:3], refs[-1]
    out_refs = refs[-1 - len(steps) : -1]
    copies = []
    for m, (joined, out_ref) in enumerate(zip(steps, out_refs)):
        for k, step in enumerate(joined):
            for g in range(out_ref.shape[0]):
                start = pl.multiple_of((g * here + (place_ref[0] ^ step)) * width, width)
                for n, field in enumerate(fields):
                    copies.append(
                        pltpu.make_async_copy(
                            field.at[:, pl.ds(start, width)],
                            out_ref.at[g, :, pl.ds((3 * k + n) * width, width)],
                            sem.at[m, k, g, n],
                        )
                    )
    for copy in copies:
        copy.start()
    for copy in copies:
        copy.wait()


def lay_out(fields, place, steps, groups, here, width, extra):
    tokens = fields[0].shape[0]
    count = len(steps)
    most = max(len(joined) for joined in steps)
    return pl.pallas_call(
        functools.partial(layout_kernel, steps, here, width),
        out_shape=[jax.ShapeDtypeStruct((groups, tokens, 3 * width * len(joined)), jnp.bfloat16) for joined in steps],
        in_specs=[SMEM] + [ANY] * (3 + len(extra)),
        out_specs=[ANY] * count,
        scratch_shapes=[pltpu.SemaphoreType.DMA((count, most, groups, 3))],
        compiler_params=limit(16),
        cost_estimate=FREE,
    )(place, *fields, *extra)


def attend_kernel(step, at_lane, width, slots, place_ref, lists_ref, counts_ref, *refs):
    qkv_ref, out_refs, held = refs[0], refs[1:-1], refs[-1]
    sources, tokens, _ = qkv_ref.shape
    member = place_ref[0] ^ step
    per = tokens // BLOCK
    scale = width ** (-0.5) * math.log2(math.e)
    q_cols, k_cols, v_cols = (slice(at_lane + n * width, at_lane + (n + 1) * width) for n in range(3))

    def rows_of(block):
        return block // per, pl.ds(pl.multiple_of((block % per) * BLOCK, BLOCK), BLOCK)

    def place_of(at):
        part = at // per
        src = part ^ place_ref[1]
        return part, src, pl.ds(pl.multiple_of((at % per) * BLOCK, BLOCK), BLOCK), src * per + at % per

    def branch(blocks):
        picked = [
            [rows_of(lists_ref[member, i * slots + j]) for j in range(2 * pairs)] for _, _, _, i, pairs in blocks
        ]

        def gathered(b, n, cols):
            return jnp.concatenate([qkv_ref[s, r, cols] for s, r in picked[b][2 * n : 2 * n + 2]], axis=0)

        scores = []
        for b, (_, src, rows, i, pairs) in enumerate(blocks):
            q = qkv_ref[src, rows, q_cols]
            found = [
                lax.dot_general(
                    q, gathered(b, n, k_cols), (((1,), (1,)), ((), ())), preferred_element_type=jnp.float32
                )
                for n in range(pairs)
            ]
            usable = BLOCK * (counts_ref[member, i] - 2 * (pairs - 1))
            column = lax.broadcasted_iota(jnp.int32, found[-1].shape, 1)
            found[-1] = jnp.where(column < usable, found[-1], -jnp.inf)
            scores.append(found)
        tops = [jnp.max(functools.reduce(jnp.maximum, found), axis=1, keepdims=True) * scale for found in scores]
        weights = [[jnp.exp2(x * scale - top) for x in found] for found, top in zip(scores, tops)]
        totals = [jnp.sum(functools.reduce(jnp.add, found), axis=1, keepdims=True) for found in weights]
        for b, (part, _, rows, _, pairs) in enumerate(blocks):
            mixed = [
                jnp.dot(weights[b][n].astype(jnp.bfloat16), gathered(b, n, v_cols), preferred_element_type=jnp.float32)
                for n in range(pairs)
            ]
            held[part, rows, :] = (functools.reduce(jnp.add, mixed) / totals[b]).astype(held.dtype)

    def two(at, carry):
        here = [place_of(2 * at), place_of(2 * at + 1)]
        pairs = [(counts_ref[member, x[3]] + 1) // 2 for x in here]
        more = pairs[0] >= pairs[1]
        first = place_of(2 * at + jnp.where(more, 0, 1))
        second = place_of(2 * at + jnp.where(more, 1, 0))
        high, low = jnp.maximum(*pairs), jnp.minimum(*pairs)
        for m in range(1, slots // 2 + 1):
            for n in range(1, m + 1):
                pl.when((high == m) & (low == n))(functools.partial(branch, [first + (m,), second + (n,)]))
        return carry

    lax.fori_loop(0, sources * per // 2, two, 0)
    each = sources // len(out_refs)
    for n, out_ref in enumerate(out_refs):
        for m in range(each):
            out_ref[m * tokens : (m + 1) * tokens, :] = held[n * each + m]


def attend(qkv, place, lists, counts, step, width, each, at_lane=0):
    sources, tokens, _ = qkv.shape
    slots = lists.shape[1] // counts.shape[1]
    return pl.pallas_call(
        functools.partial(attend_kernel, step, at_lane, width, slots),
        out_shape=[jax.ShapeDtypeStruct((each * tokens, width), jnp.bfloat16)] * (sources // each),
        in_specs=[SMEM, SMEM, SMEM, VMEM],
        out_specs=[VMEM] * (sources // each),
        scratch_shapes=[pltpu.VMEM((sources, tokens, width), jnp.bfloat16)],
        compiler_params=limit(24),
        cost_estimate=FREE,
    )(place, lists, counts, qkv)


def project_kernel(terms, n_rows, n_blocks, n_before, *refs):
    rows, blocks = refs[:n_rows], refs[n_rows : n_rows + n_blocks]
    before = refs[n_rows + n_blocks : n_rows + n_blocks + n_before]
    out_refs = refs[n_rows + n_blocks + n_before : -4]
    held, lefts, sem, row_sem = refs[-4:]
    slots = held.shape[0]
    row_copies = []
    for n, (_, picked, cut) in enumerate(terms):
        for k, r in enumerate(picked):
            wide = rows[r].shape[1]
            target = lefts.at[n, :, pl.ds(k * wide, wide)]
            row_copies.append(pltpu.make_async_copy(rows[r].at[pl.ds(cut.start, cut.stop - cut.start), :], target, row_sem.at[n, k]))
    copies = []
    for n, (pieces, _, _) in enumerate(terms):
        at = 0
        copies.append([])
        for k, piece in enumerate(pieces):
            tall = blocks[piece].shape[0]
            target = held.at[n % slots, pl.ds(at, tall), :]
            copies[-1].append(pltpu.make_async_copy(blocks[piece], target, sem.at[n % slots, k]))
            at += tall
    for copy in row_copies + sum(copies[:slots], []):
        copy.start()
    for copy in row_copies:
        copy.wait()
    step = held.shape[-1] // 4
    for n in range(len(terms)):
        for copy in copies[n]:
            copy.wait()
        left = lefts[n]
        for at in range(0, held.shape[-1], step):
            cols = slice(at, at + step)
            part = jnp.dot(left, held[n % slots, :, cols], preferred_element_type=jnp.float32)
            tall = part.shape[0] // len(out_refs)
            for m, out_ref in enumerate(out_refs):
                mine = part[m * tall : (m + 1) * tall]
                if n:
                    mine = mine + out_ref[:, cols]
                elif before:
                    mine = mine + before[m][:, cols]
                out_ref[:, cols] = mine
        if n + slots < len(terms):
            for copy in copies[n + slots]:
                copy.start()


def project(rows, blocks, terms, before, outs):
    cut = terms[0][2]
    tall = cut.stop - cut.start
    wide = blocks[0].shape[1]
    depth = sum(blocks[piece].shape[0] for piece in terms[0][0])
    slots = min(4, len(terms))
    return pl.pallas_call(
        functools.partial(project_kernel, terms, len(rows), len(blocks), len(before)),
        out_shape=[jax.ShapeDtypeStruct((tall // outs, wide), jnp.float32)] * outs,
        in_specs=[ANY] * (len(rows) + len(blocks)) + [VMEM] * len(before),
        out_specs=[VMEM] * outs,
        scratch_shapes=[
            pltpu.VMEM((slots, depth, wide), jnp.bfloat16),
            pltpu.VMEM((len(terms), tall, depth), jnp.bfloat16),
            pltpu.SemaphoreType.DMA((slots, 2)),
            pltpu.SemaphoreType.DMA((len(terms), 2)),
        ],
        compiler_params=limit(28),
        cost_estimate=FREE,
    )(*rows, *blocks, *before)


def along_z(pairs):
    return [(2 * i + c, 2 * j + c) for i, j in pairs for c in (0, 1)]


def after(value, *others):
    return lax.optimization_barrier((value, *others))[0]


def xor(p, groups):
    return [(i, i ^ p) for i in range(groups)]


UP = [(0, 1), (1, 2), (2, 3)]
DOWN = [(j, i) for i, j in UP]


def exchange(x):
    return lax.all_to_all(x, "seq", split_axis=0, concat_axis=0, tiled=True)


def shards_lines(fields, weight, rank, lists, counts, here, width):
    groups = 8
    chip = lax.axis_index("seq") // 2
    place = jnp.stack([lax.axis_index("fsdp"), rank]).astype(jnp.int32)
    n, tokens = weight.shape[0], fields[0].shape[0]

    def along(value, axis, pairs):
        return lax.ppermute(value, axis, pairs)

    def send_back(out):
        return [out[0]] + [along(out[p], "seq", xor(2 * p, groups)) for p in (1, 2, 3)]

    def attend_step(qkv, step, at_lane=0):
        return attend(qkv, place, lists, counts, step, width, 2, at_lane)

    def sides(block):
        return [along(block, "fsdp", xor(1, 4)), along(block, "fsdp", xor(2, 4))]

    def corner(x, y):
        return [along(x[:n], "fsdp", xor(2, 4)), along(y[n:], "fsdp", xor(1, 4))]

    def fence(*values):
        return lax.optimization_barrier(values)

    (x0,) = lay_out(fields, place, ((0,),), groups, here, width, [])
    qkv0 = exchange(x0)
    weight = after(weight, x0)
    up, down = along(weight, "seq", along_z(UP)), along(weight, "seq", along_z(DOWN))
    x1, x2, x3 = lay_out(fields, place, ((1,), (2,), (3,)), groups, here, width, [x0])
    up, down, qkv0, x1, x2, x3 = fence(up, down, qkv0, x1, x2, x3)
    near = jnp.concatenate([weight, jnp.where(chip % 2 == 0, down, up)], axis=0)
    qkv1 = exchange(x1)
    up2, down2 = along(up, "seq", along_z(UP[1:])), along(down, "seq", along_z(DOWN[:2]))
    near_sides = sides(near)
    out0 = attend_step(qkv0, 0)
    up2, down2, qkv1, near_sides, out0 = fence(up2, down2, qkv1, near_sides, out0)
    qkv2 = exchange(after(x2, qkv1))
    last = along(jnp.where(chip == 2, up2, down2), "seq", along_z([(1, 0), (2, 3)]))
    near_corner = [along(near, "fsdp", xor(3, 4))]
    back0 = send_back(out0)
    out1 = attend_step(qkv1, 1)
    last, qkv2, back0, near_corner = fence(last, qkv2, back0, near_corner)
    inner = (chip == 1) | (chip == 2)
    low = chip < 2
    opposite = jnp.where(inner, jnp.where(low, down, up), last)
    far = jnp.concatenate([jnp.where(low, down2, up2), opposite], axis=0)
    qkv3 = exchange(after(x3, qkv2, *out1))
    far_sides = sides(far)
    back1 = send_back(out1)
    out2 = attend_step(qkv2, 2)
    qkv3, far_sides, back1, out2 = fence(qkv3, far_sides, back1, out2)
    back2 = send_back(out2)
    far_corner = corner(*far_sides)
    out3 = attend_step(qkv3, 3)
    back0, back1, back2, out3 = fence(back0, back1, back2, out3)
    back3 = send_back(out3)

    blocks = [near] + near_sides + near_corner + [far] + far_sides + far_corner
    both, own, other = slice(0, 2 * tokens), slice(0, tokens), slice(tokens, 2 * tokens)

    def terms(step, at, cut):
        last = (7, 8) if step == 3 else (4 + step,)
        return [((step,), (4 * at, 4 * at + 1), cut), (last, (4 * at + 2, 4 * at + 3), cut)]

    early = terms(0, 0, both) + terms(1, 1, both) + terms(2, 2, both)
    mine, theirs = project(back0 + back1 + back2, blocks, early, [], 2)
    (theirs,) = project(back3, blocks, terms(3, 0, other), [theirs], 1)
    given = along(theirs.astype(jnp.bfloat16), "seq", xor(1, groups))
    (mine,) = project(back3, blocks, terms(3, 0, own), [mine], 1)
    return (mine + given.astype(jnp.float32)).astype(jnp.bfloat16)


def shards_any(fields, weight, rank, lists, counts, here, width, groups):
    place = jnp.stack([0 * rank, rank]).astype(jnp.int32)
    rows = weight.shape[0]
    gathered = lax.all_gather(weight, ("fsdp", "seq"), axis=0, tiled=True)
    gathered = gathered.reshape(here, width // rows, groups, rows, -1).transpose(0, 2, 1, 3, 4)
    gathered = gathered.reshape(here, groups, width, -1)
    ready = lay_out(fields, place, tuple((m,) for m in range(here)), groups, here, width, [])
    result = None
    for member in range(here):
        out = attend(exchange(ready[member]), place, lists, counts, member, width, 1)
        for p in range(groups):
            part = jnp.dot(
                lax.ppermute(out[p], "seq", xor(p, groups)) if p else out[0],
                lax.dynamic_index_in_dim(gathered[member], rank ^ p, 0, keepdims=False),
                preferred_element_type=jnp.float32,
            )
            result = part if result is None else result + part
    return result.astype(jnp.bfloat16)


def shards(queries, keys, values, out_weight, block_lists, block_counts):
    groups = lax.axis_size("seq")
    rank = lax.axis_index("seq")
    head_count = block_counts.shape[1]
    width = queries.shape[2] // head_count
    here = head_count // groups
    lists = lax.dynamic_slice_in_dim(block_lists[0], rank * here, here).reshape(here, -1)
    counts = lax.dynamic_slice_in_dim(block_counts[0], rank * here, here)
    fields = [x[0] for x in (queries, keys, values)]
    if groups == 8 and here == 4 and lax.axis_size("fsdp") == 4 and out_weight.shape[0] == width:
        result = shards_lines(fields, out_weight, rank, lists, counts, here, width)
    else:
        result = shards_any(fields, out_weight, rank, lists, counts, here, width, groups)
    return result[None]


def solution(mesh):
    return jax.shard_map(
        shards,
        mesh=mesh,
        in_specs=(
            P("fsdp", "seq", None),
            P("fsdp", "seq", None),
            P("fsdp", "seq", None),
            P(("seq", "fsdp"), None),
            P("fsdp", None, None, None),
            P("fsdp", None, None),
        ),
        out_specs=P("fsdp", "seq", None),
        check_vma=False,
    )
```

```python
import functools
import math

import jax
import jax.numpy as jnp
from jax import lax
from jax.experimental import pallas as pl
from jax.experimental.pallas import tpu as pltpu
from jax.sharding import PartitionSpec as P

BLOCK = 128
VMEM = pl.BlockSpec(memory_space=pltpu.VMEM)
SMEM = pl.BlockSpec(memory_space=pltpu.SMEM)
ANY = pl.BlockSpec(memory_space=pl.ANY)
FREE = pl.CostEstimate(flops=1, bytes_accessed=1, transcendentals=0)


def limit(mib):
    return pltpu.CompilerParams(vmem_limit_bytes=mib * 1024 * 1024)


def layout_kernel(steps, here, width, place_ref, *refs):
    fields, sem = refs[:3], refs[-1]
    out_refs = refs[-1 - len(steps) : -1]
    copies = []
    for m, (joined, out_ref) in enumerate(zip(steps, out_refs)):
        for k, step in enumerate(joined):
            for g in range(out_ref.shape[0]):
                start = pl.multiple_of((g * here + (place_ref[0] ^ step)) * width, width)
                for n, field in enumerate(fields):
                    copies.append(
                        pltpu.make_async_copy(
                            field.at[:, pl.ds(start, width)],
                            out_ref.at[g, :, pl.ds((3 * k + n) * width, width)],
                            sem.at[m, k, g, n],
                        )
                    )
    for copy in copies:
        copy.start()
    for copy in copies:
        copy.wait()


def lay_out(fields, place, steps, groups, here, width, extra):
    tokens = fields[0].shape[0]
    count = len(steps)
    most = max(len(joined) for joined in steps)
    return pl.pallas_call(
        functools.partial(layout_kernel, steps, here, width),
        out_shape=[jax.ShapeDtypeStruct((groups, tokens, 3 * width * len(joined)), jnp.bfloat16) for joined in steps],
        in_specs=[SMEM] + [ANY] * (3 + len(extra)),
        out_specs=[VMEM] * count,
        scratch_shapes=[pltpu.SemaphoreType.DMA((count, most, groups, 3))],
        compiler_params=limit(56),
        cost_estimate=FREE,
    )(place, *fields, *extra)


def attend_kernel(step, at_lane, width, slots, place_ref, lists_ref, counts_ref, *refs):
    qkv_ref, out_refs, held = refs[0], refs[1:-1], refs[-1]
    sources, tokens, _ = qkv_ref.shape
    member = place_ref[0] ^ step
    per = tokens // BLOCK
    scale = width ** (-0.5) * math.log2(math.e)
    q_cols, k_cols, v_cols = (slice(at_lane + n * width, at_lane + (n + 1) * width) for n in range(3))

    def rows_of(block):
        return block // per, pl.ds(pl.multiple_of((block % per) * BLOCK, BLOCK), BLOCK)

    def place_of(at):
        part = at // per
        src = part ^ place_ref[1]
        return part, src, pl.ds(pl.multiple_of((at % per) * BLOCK, BLOCK), BLOCK), src * per + at % per

    def branch(blocks):
        picked = [
            [rows_of(lists_ref[member, i * slots + j]) for j in range(2 * pairs)] for _, _, _, i, pairs in blocks
        ]

        def gathered(b, n, cols):
            return jnp.concatenate([qkv_ref[s, r, cols] for s, r in picked[b][2 * n : 2 * n + 2]], axis=0)

        scores = []
        for b, (_, src, rows, i, pairs) in enumerate(blocks):
            q = qkv_ref[src, rows, q_cols]
            found = [
                lax.dot_general(
                    q, gathered(b, n, k_cols), (((1,), (1,)), ((), ())), preferred_element_type=jnp.float32
                )
                for n in range(pairs)
            ]
            usable = BLOCK * (counts_ref[member, i] - 2 * (pairs - 1))
            column = lax.broadcasted_iota(jnp.int32, found[-1].shape, 1)
            found[-1] = jnp.where(column < usable, found[-1], -jnp.inf)
            scores.append(found)
        tops = [jnp.max(functools.reduce(jnp.maximum, found), axis=1, keepdims=True) * scale for found in scores]
        weights = [[jnp.exp2(x * scale - top) for x in found] for found, top in zip(scores, tops)]
        totals = [jnp.sum(functools.reduce(jnp.add, found), axis=1, keepdims=True) for found in weights]
        for b, (part, _, rows, _, pairs) in enumerate(blocks):
            mixed = [
                jnp.dot(weights[b][n].astype(jnp.bfloat16), gathered(b, n, v_cols), preferred_element_type=jnp.float32)
                for n in range(pairs)
            ]
            held[part, rows, :] = (functools.reduce(jnp.add, mixed) / totals[b]).astype(held.dtype)

    def two(at, carry):
        here = [place_of(2 * at), place_of(2 * at + 1)]
        pairs = [(counts_ref[member, x[3]] + 1) // 2 for x in here]
        more = pairs[0] >= pairs[1]
        first = place_of(2 * at + jnp.where(more, 0, 1))
        second = place_of(2 * at + jnp.where(more, 1, 0))
        high, low = jnp.maximum(*pairs), jnp.minimum(*pairs)
        for m in range(1, slots // 2 + 1):
            for n in range(1, m + 1):
                pl.when((high == m) & (low == n))(functools.partial(branch, [first + (m,), second + (n,)]))
        return carry

    lax.fori_loop(0, sources * per // 2, two, 0)
    each = sources // len(out_refs)
    for n, out_ref in enumerate(out_refs):
        for m in range(each):
            out_ref[m * tokens : (m + 1) * tokens, :] = held[n * each + m]


def attend(qkv, place, lists, counts, step, width, each, at_lane=0):
    sources, tokens, _ = qkv.shape
    slots = lists.shape[1] // counts.shape[1]
    return pl.pallas_call(
        functools.partial(attend_kernel, step, at_lane, width, slots),
        out_shape=[jax.ShapeDtypeStruct((each * tokens, width), jnp.bfloat16)] * (sources // each),
        in_specs=[SMEM, SMEM, SMEM, VMEM],
        out_specs=[VMEM] * (sources // each),
        scratch_shapes=[pltpu.VMEM((sources, tokens, width), jnp.bfloat16)],
        compiler_params=limit(12),
        cost_estimate=FREE,
    )(place, lists, counts, qkv)


def project_kernel(terms, n_rows, n_blocks, n_before, *refs):
    rows, blocks = refs[:n_rows], refs[n_rows : n_rows + n_blocks]
    before = refs[n_rows + n_blocks : n_rows + n_blocks + n_before]
    out_refs = refs[n_rows + n_blocks + n_before : -4]
    held, lefts, sem, row_sem = refs[-4:]
    slots = held.shape[0]
    row_copies = []
    for n, (_, picked, cut) in enumerate(terms):
        for k, (r, lane) in enumerate(picked):
            wide = lefts.shape[2] // len(picked)
            source = rows[r].at[pl.ds(cut.start, cut.stop - cut.start), pl.ds(lane, wide)]
            target = lefts.at[n, :, pl.ds(k * wide, wide)]
            row_copies.append(pltpu.make_async_copy(source, target, row_sem.at[n, k]))
    copies = []
    for n, (pieces, _, _) in enumerate(terms):
        at = 0
        copies.append([])
        for k, piece in enumerate(pieces):
            tall = blocks[piece].shape[0]
            target = held.at[n % slots, pl.ds(at, tall), :]
            copies[-1].append(pltpu.make_async_copy(blocks[piece], target, sem.at[n % slots, k]))
            at += tall
    for copy in row_copies + sum(copies[:slots], []):
        copy.start()
    for copy in row_copies:
        copy.wait()
    step = held.shape[-1] // 4
    for n in range(len(terms)):
        for copy in copies[n]:
            copy.wait()
        left = lefts[n]
        for at in range(0, held.shape[-1], step):
            cols = slice(at, at + step)
            part = jnp.dot(left, held[n % slots, :, cols], preferred_element_type=jnp.float32)
            tall = part.shape[0] // len(out_refs)
            for m, out_ref in enumerate(out_refs):
                mine = part[m * tall : (m + 1) * tall]
                if n:
                    mine = mine + out_ref[:, cols]
                elif before:
                    mine = mine + before[m][:, cols]
                out_ref[:, cols] = mine
        if n + slots < len(terms):
            for copy in copies[n + slots]:
                copy.start()


def project(rows, blocks, terms, before, outs):
    cut = terms[0][2]
    tall = cut.stop - cut.start
    wide = blocks[0].shape[1]
    depth = sum(blocks[piece].shape[0] for piece in terms[0][0])
    slots = min(4, len(terms))
    return pl.pallas_call(
        functools.partial(project_kernel, terms, len(rows), len(blocks), len(before)),
        out_shape=[jax.ShapeDtypeStruct((tall // outs, wide), jnp.float32)] * outs,
        in_specs=[ANY] * (len(rows) + len(blocks)) + [VMEM] * len(before),
        out_specs=[VMEM] * outs,
        scratch_shapes=[
            pltpu.VMEM((slots, depth, wide), jnp.bfloat16),
            pltpu.VMEM((len(terms), tall, depth), jnp.bfloat16),
            pltpu.SemaphoreType.DMA((slots, 2)),
            pltpu.SemaphoreType.DMA((len(terms), 2)),
        ],
        compiler_params=limit(36),
        cost_estimate=FREE,
    )(*rows, *blocks, *before)


def along_z(pairs):
    return [(2 * i + c, 2 * j + c) for i, j in pairs for c in (0, 1)]


def after(value, *others):
    return lax.optimization_barrier((value, *others))[0]


def xor(p, groups):
    return [(i, i ^ p) for i in range(groups)]


UP = [(0, 1), (1, 2), (2, 3)]
DOWN = [(j, i) for i, j in UP]


def exchange(x):
    return lax.all_to_all(x, "seq", split_axis=0, concat_axis=0, tiled=True)


def shards_lines(fields, weight, rank, lists, counts, here, width):
    groups = 8
    chip = lax.axis_index("seq") // 2
    place = jnp.stack([lax.axis_index("fsdp"), rank]).astype(jnp.int32)
    n, tokens = weight.shape[0], fields[0].shape[0]

    both = slice(0, 2 * tokens)

    def along(value, axis, pairs):
        return lax.ppermute(value, axis, pairs)

    def send_back(out):
        return [out[0]] + [along(out[p], "seq", xor(2 * p, groups)) for p in (1, 2, 3)]

    def attend_step(qkv, step, at_lane=0):
        return attend(qkv, place, lists, counts, step, width, 2, at_lane)

    def sides(block):
        return [along(block, "fsdp", xor(1, 4)), along(block, "fsdp", xor(2, 4))]

    def corner(x, y):
        return [along(x[:n], "fsdp", xor(2, 4)), along(y[n:], "fsdp", xor(1, 4))]

    def fence(*values):
        return lax.optimization_barrier(values)

    (x0,) = lay_out(fields, place, ((0,),), groups, here, width, [])
    qkv0 = exchange(x0)
    up, down = along(weight, "seq", along_z(UP)), along(weight, "seq", along_z(DOWN))
    x1, x2, x3 = lay_out(fields, place, ((1,), (2,), (3,)), groups, here, width, [x0])
    up, down, qkv0, x1, x2, x3 = fence(up, down, qkv0, x1, x2, x3)
    near = jnp.concatenate([weight, jnp.where(chip % 2 == 0, down, up)], axis=0)
    qkv1 = exchange(x1)
    up2, down2 = along(up, "seq", along_z(UP[1:])), along(down, "seq", along_z(DOWN[:2]))
    near_sides = sides(near)
    out0 = attend_step(qkv0, 0)
    up2, down2, qkv1, near_sides, out0 = fence(up2, down2, qkv1, near_sides, out0)
    qkv2 = exchange(after(x2, qkv1))
    last = along(jnp.where(chip == 2, up2, down2), "seq", along_z([(1, 0), (2, 3)]))
    near_corner = [along(near, "fsdp", xor(3, 4))]
    back0 = send_back(out0)
    out1 = attend_step(qkv1, 1)
    last, qkv2, back0, near_corner = fence(last, qkv2, back0, near_corner)
    inner = (chip == 1) | (chip == 2)
    low = chip < 2
    opposite = jnp.where(inner, jnp.where(low, down, up), last)
    far = jnp.concatenate([jnp.where(low, down2, up2), opposite], axis=0)
    qkv3 = exchange(after(x3, qkv2, *out1))
    far_sides = sides(far)
    back1 = send_back(out1)
    out2 = attend_step(qkv2, 2)
    joined = jnp.concatenate(back0, axis=1)
    qkv3, far_sides, back1, out2, joined = fence(qkv3, far_sides, back1, out2, joined)
    back2 = send_back(out2)
    out3 = attend_step(qkv3, 3)
    far_corner = corner(*far_sides)
    back3 = [out3[0], None] + [along(out3[p], "seq", xor(2 * p, groups)) for p in (2, 3)]
    back2, side = fence(back2, out3[1])
    back3[1] = along(side, "seq", xor(2, groups))

    sides_all = [near] + near_sides + [far] + far_sides
    rows = [joined] + back1 + back2
    early = [((0,), ((0, 0),), both), ((3,), ((0, 2 * width),), both)]
    for m in (1, 2):
        for h in (0, 1):
            at = 4 * m - 3 + 2 * h
            early.append(((m + 3 * h,), ((at, 0), (at + 1, 0)), both))
    mine, theirs = project(rows, sides_all, early, [], 2)

    def finish(cut, before):
        near_pieces = tuple(range(len(near_corner)))
        far_pieces = tuple(range(len(near_corner), len(near_corner + far_corner)))
        terms = [(near_pieces, ((0, 0), (1, 0)), cut), (far_pieces, ((2, 0), (3, 0)), cut)]
        return project(back3, near_corner + far_corner, terms, [before], 1)[0]

    theirs = finish(slice(tokens, 2 * tokens), theirs)
    given = along(theirs.astype(jnp.bfloat16), "seq", xor(1, groups))
    mine = finish(slice(0, tokens), mine)
    return (mine + given.astype(jnp.float32)).astype(jnp.bfloat16)


def shards_any(fields, weight, rank, lists, counts, here, width, groups):
    place = jnp.stack([0 * rank, rank]).astype(jnp.int32)
    rows = weight.shape[0]
    gathered = lax.all_gather(weight, ("fsdp", "seq"), axis=0, tiled=True)
    gathered = gathered.reshape(here, width // rows, groups, rows, -1).transpose(0, 2, 1, 3, 4)
    gathered = gathered.reshape(here, groups, width, -1)
    ready = lay_out(fields, place, tuple((m,) for m in range(here)), groups, here, width, [])
    result = None
    for member in range(here):
        out = attend(exchange(ready[member]), place, lists, counts, member, width, 1)
        for p in range(groups):
            part = jnp.dot(
                lax.ppermute(out[p], "seq", xor(p, groups)) if p else out[0],
                lax.dynamic_index_in_dim(gathered[member], rank ^ p, 0, keepdims=False),
                preferred_element_type=jnp.float32,
            )
            result = part if result is None else result + part
    return result.astype(jnp.bfloat16)


def shards(queries, keys, values, out_weight, block_lists, block_counts):
    groups = lax.axis_size("seq")
    rank = lax.axis_index("seq")
    head_count = block_counts.shape[1]
    width = queries.shape[2] // head_count
    here = head_count // groups
    lists = lax.dynamic_slice_in_dim(block_lists[0], rank * here, here).reshape(here, -1)
    counts = lax.dynamic_slice_in_dim(block_counts[0], rank * here, here)
    fields = [x[0] for x in (queries, keys, values)]
    if groups == 8 and here == 4 and lax.axis_size("fsdp") == 4 and out_weight.shape[0] == width:
        result = shards_lines(fields, out_weight, rank, lists, counts, here, width)
    else:
        result = shards_any(fields, out_weight, rank, lists, counts, here, width, groups)
    return result[None]


def solution(mesh):
    return jax.shard_map(
        shards,
        mesh=mesh,
        in_specs=(
            P("fsdp", "seq", None),
            P("fsdp", "seq", None),
            P("fsdp", "seq", None),
            P(("seq", "fsdp"), None),
            P("fsdp", None, None, None),
            P("fsdp", None, None),
        ),
        out_specs=P("fsdp", "seq", None),
        check_vma=False,
    )
```

```python
import functools
import math

import jax
import jax.numpy as jnp
from jax import lax
from jax.experimental import pallas as pl
from jax.experimental.pallas import tpu as pltpu
from jax.sharding import PartitionSpec as P

BLOCK = 128
VMEM = pl.BlockSpec(memory_space=pltpu.VMEM)
SMEM = pl.BlockSpec(memory_space=pltpu.SMEM)
ANY = pl.BlockSpec(memory_space=pl.ANY)
FREE = pl.CostEstimate(flops=1, bytes_accessed=1, transcendentals=0)


def limit(mib):
    return pltpu.CompilerParams(vmem_limit_bytes=mib * 1024 * 1024)


def layout_kernel(steps, here, width, place_ref, *refs):
    fields, sem = refs[:3], refs[-1]
    out_refs = refs[-1 - len(steps) : -1]
    copies = []
    for m, (joined, out_ref) in enumerate(zip(steps, out_refs)):
        for k, step in enumerate(joined):
            for g in range(out_ref.shape[0]):
                start = pl.multiple_of((g * here + (place_ref[0] ^ step)) * width, width)
                for n, field in enumerate(fields):
                    copies.append(
                        pltpu.make_async_copy(
                            field.at[:, pl.ds(start, width)],
                            out_ref.at[g, :, pl.ds((3 * k + n) * width, width)],
                            sem.at[m, k, g, n],
                        )
                    )
    for copy in copies:
        copy.start()
    for copy in copies:
        copy.wait()


def lay_out(fields, place, steps, groups, here, width, extra):
    tokens = fields[0].shape[0]
    count = len(steps)
    most = max(len(joined) for joined in steps)
    return pl.pallas_call(
        functools.partial(layout_kernel, steps, here, width),
        out_shape=[jax.ShapeDtypeStruct((groups, tokens, 3 * width * len(joined)), jnp.bfloat16) for joined in steps],
        in_specs=[SMEM] + [ANY] * (3 + len(extra)),
        out_specs=[VMEM] * count,
        scratch_shapes=[pltpu.SemaphoreType.DMA((count, most, groups, 3))],
        compiler_params=limit(56),
        cost_estimate=FREE,
    )(place, *fields, *extra)


def attend_kernel(step, at_lane, width, slots, place_ref, lists_ref, counts_ref, *refs):
    qkv_ref, out_refs, held = refs[0], refs[1:-1], refs[-1]
    sources, tokens, _ = qkv_ref.shape
    member = place_ref[0] ^ step
    per = tokens // BLOCK
    scale = width ** (-0.5) * math.log2(math.e)
    q_cols, k_cols, v_cols = (slice(at_lane + n * width, at_lane + (n + 1) * width) for n in range(3))

    def rows_of(block):
        return block // per, pl.ds(pl.multiple_of((block % per) * BLOCK, BLOCK), BLOCK)

    def place_of(at):
        part = at // per
        src = part ^ place_ref[1]
        return part, src, pl.ds(pl.multiple_of((at % per) * BLOCK, BLOCK), BLOCK), src * per + at % per

    def branch(blocks):
        picked = [
            [rows_of(lists_ref[member, i * slots + j]) for j in range(2 * pairs)] for _, _, _, i, pairs in blocks
        ]

        def gathered(b, n, cols):
            return jnp.concatenate([qkv_ref[s, r, cols] for s, r in picked[b][2 * n : 2 * n + 2]], axis=0)

        scores = []
        for b, (_, src, rows, i, pairs) in enumerate(blocks):
            q = qkv_ref[src, rows, q_cols]
            found = [
                lax.dot_general(
                    q, gathered(b, n, k_cols), (((1,), (1,)), ((), ())), preferred_element_type=jnp.float32
                )
                for n in range(pairs)
            ]
            usable = BLOCK * (counts_ref[member, i] - 2 * (pairs - 1))
            column = lax.broadcasted_iota(jnp.int32, found[-1].shape, 1)
            found[-1] = jnp.where(column < usable, found[-1], -jnp.inf)
            scores.append(found)
        tops = [jnp.max(functools.reduce(jnp.maximum, found), axis=1, keepdims=True) * scale for found in scores]
        weights = [[jnp.exp2(x * scale - top) for x in found] for found, top in zip(scores, tops)]
        totals = [jnp.sum(functools.reduce(jnp.add, found), axis=1, keepdims=True) for found in weights]
        for b, (part, _, rows, _, pairs) in enumerate(blocks):
            mixed = [
                jnp.dot(weights[b][n].astype(jnp.bfloat16), gathered(b, n, v_cols), preferred_element_type=jnp.float32)
                for n in range(pairs)
            ]
            held[part, rows, :] = (functools.reduce(jnp.add, mixed) / totals[b]).astype(held.dtype)

    def two(at, carry):
        here = [place_of(2 * at), place_of(2 * at + 1)]
        pairs = [(counts_ref[member, x[3]] + 1) // 2 for x in here]
        more = pairs[0] >= pairs[1]
        first = place_of(2 * at + jnp.where(more, 0, 1))
        second = place_of(2 * at + jnp.where(more, 1, 0))
        high, low = jnp.maximum(*pairs), jnp.minimum(*pairs)
        for m in range(1, slots // 2 + 1):
            for n in range(1, m + 1):
                pl.when((high == m) & (low == n))(functools.partial(branch, [first + (m,), second + (n,)]))
        return carry

    lax.fori_loop(0, sources * per // 2, two, 0)
    each = sources // len(out_refs)
    for n, out_ref in enumerate(out_refs):
        for m in range(each):
            out_ref[m * tokens : (m + 1) * tokens, :] = held[n * each + m]


def attend(qkv, place, lists, counts, step, width, each, at_lane=0):
    sources, tokens, _ = qkv.shape
    slots = lists.shape[1] // counts.shape[1]
    return pl.pallas_call(
        functools.partial(attend_kernel, step, at_lane, width, slots),
        out_shape=[jax.ShapeDtypeStruct((each * tokens, width), jnp.bfloat16)] * (sources // each),
        in_specs=[SMEM, SMEM, SMEM, VMEM],
        out_specs=[VMEM] * (sources // each),
        scratch_shapes=[pltpu.VMEM((sources, tokens, width), jnp.bfloat16)],
        compiler_params=limit(12),
        cost_estimate=FREE,
    )(place, lists, counts, qkv)


def project_kernel(terms, n_rows, n_blocks, n_before, *refs):
    rows, blocks = refs[:n_rows], refs[n_rows : n_rows + n_blocks]
    before = refs[n_rows + n_blocks : n_rows + n_blocks + n_before]
    out_refs = refs[n_rows + n_blocks + n_before : -4]
    held, lefts, sem, row_sem = refs[-4:]
    slots = held.shape[0]
    row_copies = []
    for n, (_, picked, cut) in enumerate(terms):
        for k, (r, lane) in enumerate(picked):
            wide = lefts.shape[2] // len(picked)
            source = rows[r].at[pl.ds(cut.start, cut.stop - cut.start), pl.ds(lane, wide)]
            target = lefts.at[n, :, pl.ds(k * wide, wide)]
            row_copies.append(pltpu.make_async_copy(source, target, row_sem.at[n, k]))
    copies = []
    for n, (pieces, _, _) in enumerate(terms):
        at = 0
        copies.append([])
        for k, piece in enumerate(pieces):
            tall = blocks[piece].shape[0]
            target = held.at[n % slots, pl.ds(at, tall), :]
            copies[-1].append(pltpu.make_async_copy(blocks[piece], target, sem.at[n % slots, k]))
            at += tall
    for copy in row_copies + sum(copies[:slots], []):
        copy.start()
    for copy in row_copies:
        copy.wait()
    step = held.shape[-1] // 4
    for n in range(len(terms)):
        for copy in copies[n]:
            copy.wait()
        left = lefts[n]
        for at in range(0, held.shape[-1], step):
            cols = slice(at, at + step)
            part = jnp.dot(left, held[n % slots, :, cols], preferred_element_type=jnp.float32)
            tall = part.shape[0] // len(out_refs)
            for m, out_ref in enumerate(out_refs):
                mine = part[m * tall : (m + 1) * tall]
                if n:
                    mine = mine + out_ref[:, cols]
                elif before:
                    mine = mine + before[m][:, cols]
                out_ref[:, cols] = mine
        if n + slots < len(terms):
            for copy in copies[n + slots]:
                copy.start()


def project(rows, blocks, terms, before, outs):
    cut = terms[0][2]
    tall = cut.stop - cut.start
    wide = blocks[0].shape[1]
    depth = sum(blocks[piece].shape[0] for piece in terms[0][0])
    slots = min(4, len(terms))
    return pl.pallas_call(
        functools.partial(project_kernel, terms, len(rows), len(blocks), len(before)),
        out_shape=[jax.ShapeDtypeStruct((tall // outs, wide), jnp.float32)] * outs,
        in_specs=[ANY] * (len(rows) + len(blocks)) + [VMEM] * len(before),
        out_specs=[VMEM] * outs,
        scratch_shapes=[
            pltpu.VMEM((slots, depth, wide), jnp.bfloat16),
            pltpu.VMEM((len(terms), tall, depth), jnp.bfloat16),
            pltpu.SemaphoreType.DMA((slots, 2)),
            pltpu.SemaphoreType.DMA((len(terms), 2)),
        ],
        compiler_params=limit(36),
        cost_estimate=FREE,
    )(*rows, *blocks, *before)


def along_z(pairs):
    return [(2 * i + c, 2 * j + c) for i, j in pairs for c in (0, 1)]


def after(value, *others):
    return lax.optimization_barrier((value, *others))[0]


def xor(p, groups):
    return [(i, i ^ p) for i in range(groups)]


UP = [(0, 1), (1, 2), (2, 3)]
DOWN = [(j, i) for i, j in UP]


def exchange(x):
    return lax.all_to_all(x, "seq", split_axis=0, concat_axis=0, tiled=True)


def shards_lines(fields, weight, rank, lists, counts, here, width):
    groups = 8
    chip = lax.axis_index("seq") // 2
    place = jnp.stack([lax.axis_index("fsdp"), rank]).astype(jnp.int32)
    n, tokens = weight.shape[0], fields[0].shape[0]

    both = slice(0, 2 * tokens)

    def along(value, axis, pairs):
        return lax.ppermute(value, axis, pairs)

    def send_back(out):
        return [out[0]] + [along(out[p], "seq", xor(2 * p, groups)) for p in (1, 2, 3)]

    def attend_step(qkv, step, at_lane=0):
        return attend(qkv, place, lists, counts, step, width, 2, at_lane)

    def sides(block):
        return [along(block, "fsdp", xor(1, 4)), along(block, "fsdp", xor(2, 4))]

    def fence(*values):
        return lax.optimization_barrier(values)

    (x0,) = lay_out(fields, place, ((0,),), groups, here, width, [])
    qkv0 = exchange(x0)
    up, down = along(weight, "seq", along_z(UP)), along(weight, "seq", along_z(DOWN))
    x1, x2, x3 = lay_out(fields, place, ((1,), (2,), (3,)), groups, here, width, [x0])
    up, down, qkv0, x1, x2, x3 = fence(up, down, qkv0, x1, x2, x3)
    near = jnp.concatenate([weight, jnp.where(chip % 2 == 0, down, up)], axis=0)
    qkv1 = exchange(x1)
    up2, down2 = along(up, "seq", along_z(UP[1:])), along(down, "seq", along_z(DOWN[:2]))
    near_sides = sides(near)
    out0 = attend_step(qkv0, 0)
    up2, down2, qkv1, near_sides, out0 = fence(up2, down2, qkv1, near_sides, out0)
    qkv2 = exchange(after(x2, qkv1))
    last = along(jnp.where(chip == 2, up2, down2), "seq", along_z([(1, 0), (2, 3)]))
    near_corner = [along(near, "fsdp", xor(3, 4))]
    back0 = send_back(out0)
    out1 = attend_step(qkv1, 1)
    last, qkv2, back0, near_corner = fence(last, qkv2, back0, near_corner)
    inner = (chip == 1) | (chip == 2)
    low = chip < 2
    opposite = jnp.where(inner, jnp.where(low, down, up), last)
    far = jnp.concatenate([jnp.where(low, down2, up2), opposite], axis=0)
    qkv3 = exchange(after(x3, qkv2, *out1))
    far_sides = sides(far)
    back1 = send_back(out1)
    out2 = attend_step(qkv2, 2)
    joined = jnp.concatenate(back0, axis=1)
    halves = [far_sides[0][:n], far_sides[1][n:]]
    qkv3, far_sides, halves, back1, out2, joined = fence(qkv3, far_sides, halves, back1, out2, joined)
    joined1 = jnp.concatenate(back1, axis=1)
    back2 = send_back(out2)
    out3 = attend_step(qkv3, 3)
    far_corner = [along(halves[0], "fsdp", xor(2, 4)), along(halves[1], "fsdp", xor(1, 4))]
    back2, out3 = fence(back2, out3)
    back3 = send_back(out3)

    sides_all = [near] + near_sides + [far] + far_sides
    rows = [joined, joined1] + back2
    early = [((0,), ((0, 0),), both), ((3,), ((0, 2 * width),), both)]
    early += [((1,), ((1, 0),), both), ((4,), ((1, 2 * width),), both)]
    early += [((2,), ((2, 0), (3, 0)), both), ((5,), ((4, 0), (5, 0)), both)]
    mine, theirs = project(rows, sides_all, early, [], 2)

    def finish(cut, before):
        near_pieces = tuple(range(len(near_corner)))
        far_pieces = tuple(range(len(near_corner), len(near_corner + far_corner)))
        terms = [(near_pieces, ((0, 0), (1, 0)), cut), (far_pieces, ((2, 0), (3, 0)), cut)]
        return project(back3, near_corner + far_corner, terms, [before], 1)[0]

    theirs = finish(slice(tokens, 2 * tokens), theirs)
    given = along(theirs.astype(jnp.bfloat16), "seq", xor(1, groups))
    mine = finish(slice(0, tokens), mine)
    return (mine + given.astype(jnp.float32)).astype(jnp.bfloat16)


def shards_any(fields, weight, rank, lists, counts, here, width, groups):
    place = jnp.stack([0 * rank, rank]).astype(jnp.int32)
    rows = weight.shape[0]
    gathered = lax.all_gather(weight, ("fsdp", "seq"), axis=0, tiled=True)
    gathered = gathered.reshape(here, width // rows, groups, rows, -1).transpose(0, 2, 1, 3, 4)
    gathered = gathered.reshape(here, groups, width, -1)
    ready = lay_out(fields, place, tuple((m,) for m in range(here)), groups, here, width, [])
    result = None
    for member in range(here):
        out = attend(exchange(ready[member]), place, lists, counts, member, width, 1)
        for p in range(groups):
            part = jnp.dot(
                lax.ppermute(out[p], "seq", xor(p, groups)) if p else out[0],
                lax.dynamic_index_in_dim(gathered[member], rank ^ p, 0, keepdims=False),
                preferred_element_type=jnp.float32,
            )
            result = part if result is None else result + part
    return result.astype(jnp.bfloat16)


def shards(queries, keys, values, out_weight, block_lists, block_counts):
    groups = lax.axis_size("seq")
    rank = lax.axis_index("seq")
    head_count = block_counts.shape[1]
    width = queries.shape[2] // head_count
    here = head_count // groups
    lists = lax.dynamic_slice_in_dim(block_lists[0], rank * here, here).reshape(here, -1)
    counts = lax.dynamic_slice_in_dim(block_counts[0], rank * here, here)
    fields = [x[0] for x in (queries, keys, values)]
    if groups == 8 and here == 4 and lax.axis_size("fsdp") == 4 and out_weight.shape[0] == width:
        result = shards_lines(fields, out_weight, rank, lists, counts, here, width)
    else:
        result = shards_any(fields, out_weight, rank, lists, counts, here, width, groups)
    return result[None]


def solution(mesh):
    return jax.shard_map(
        shards,
        mesh=mesh,
        in_specs=(
            P("fsdp", "seq", None),
            P("fsdp", "seq", None),
            P("fsdp", "seq", None),
            P(("seq", "fsdp"), None),
            P("fsdp", None, None, None),
            P("fsdp", None, None),
        ),
        out_specs=P("fsdp", "seq", None),
        check_vma=False,
    )
```

```python
import functools
import math

import jax
import jax.numpy as jnp
from jax import lax
from jax.experimental import pallas as pl
from jax.experimental.pallas import tpu as pltpu
from jax.sharding import PartitionSpec as P

BLOCK = 128
VMEM = pl.BlockSpec(memory_space=pltpu.VMEM)
SMEM = pl.BlockSpec(memory_space=pltpu.SMEM)
ANY = pl.BlockSpec(memory_space=pl.ANY)
FREE = pl.CostEstimate(flops=1, bytes_accessed=1, transcendentals=0)


def limit(mib):
    return pltpu.CompilerParams(vmem_limit_bytes=mib * 1024 * 1024)


def layout_kernel(steps, here, width, place_ref, *refs):
    fields, sem = refs[:3], refs[-1]
    out_refs = refs[-1 - len(steps) : -1]
    copies = []
    for m, (joined, out_ref) in enumerate(zip(steps, out_refs)):
        for k, step in enumerate(joined):
            for g in range(out_ref.shape[0]):
                start = pl.multiple_of((g * here + (place_ref[0] ^ step)) * width, width)
                for n, field in enumerate(fields):
                    copies.append(
                        pltpu.make_async_copy(
                            field.at[:, pl.ds(start, width)],
                            out_ref.at[g, :, pl.ds((3 * k + n) * width, width)],
                            sem.at[m, k, g, n],
                        )
                    )
    for copy in copies:
        copy.start()
    for copy in copies:
        copy.wait()


def lay_out(fields, place, steps, groups, here, width, extra):
    tokens = fields[0].shape[0]
    count = len(steps)
    most = max(len(joined) for joined in steps)
    return pl.pallas_call(
        functools.partial(layout_kernel, steps, here, width),
        out_shape=[jax.ShapeDtypeStruct((groups, tokens, 3 * width * len(joined)), jnp.bfloat16) for joined in steps],
        in_specs=[SMEM] + [ANY] * (3 + len(extra)),
        out_specs=[VMEM] * count,
        scratch_shapes=[pltpu.SemaphoreType.DMA((count, most, groups, 3))],
        compiler_params=limit(56),
        cost_estimate=FREE,
    )(place, *fields, *extra)


def attend_kernel(step, at_lane, width, slots, place_ref, lists_ref, counts_ref, *refs):
    qkv_ref, out_refs, held = refs[0], refs[1:-1], refs[-1]
    sources, tokens, _ = qkv_ref.shape
    member = place_ref[0] ^ step
    per = tokens // BLOCK
    scale = width ** (-0.5) * math.log2(math.e)
    q_cols, k_cols, v_cols = (slice(at_lane + n * width, at_lane + (n + 1) * width) for n in range(3))

    def rows_of(block):
        return block // per, pl.ds(pl.multiple_of((block % per) * BLOCK, BLOCK), BLOCK)

    def place_of(at):
        part = at // per
        src = part ^ place_ref[1]
        return part, src, pl.ds(pl.multiple_of((at % per) * BLOCK, BLOCK), BLOCK), src * per + at % per

    def branch(blocks):
        picked = [
            [rows_of(lists_ref[member, i * slots + j]) for j in range(2 * pairs)] for _, _, _, i, pairs in blocks
        ]

        def gathered(b, n, cols):
            return jnp.concatenate([qkv_ref[s, r, cols] for s, r in picked[b][2 * n : 2 * n + 2]], axis=0)

        scores = []
        for b, (_, src, rows, i, pairs) in enumerate(blocks):
            q = qkv_ref[src, rows, q_cols]
            found = [
                lax.dot_general(
                    q, gathered(b, n, k_cols), (((1,), (1,)), ((), ())), preferred_element_type=jnp.float32
                )
                for n in range(pairs)
            ]
            usable = BLOCK * (counts_ref[member, i] - 2 * (pairs - 1))
            column = lax.broadcasted_iota(jnp.int32, found[-1].shape, 1)
            found[-1] = jnp.where(column < usable, found[-1], -jnp.inf)
            scores.append(found)
        tops = [jnp.max(functools.reduce(jnp.maximum, found), axis=1, keepdims=True) * scale for found in scores]
        weights = [[jnp.exp2(x * scale - top) for x in found] for found, top in zip(scores, tops)]
        totals = [jnp.sum(functools.reduce(jnp.add, found), axis=1, keepdims=True) for found in weights]
        for b, (part, _, rows, _, pairs) in enumerate(blocks):
            mixed = [
                jnp.dot(weights[b][n].astype(jnp.bfloat16), gathered(b, n, v_cols), preferred_element_type=jnp.float32)
                for n in range(pairs)
            ]
            held[part, rows, :] = (functools.reduce(jnp.add, mixed) / totals[b]).astype(held.dtype)

    def two(at, carry):
        here = [place_of(2 * at), place_of(2 * at + 1)]
        pairs = [(counts_ref[member, x[3]] + 1) // 2 for x in here]
        more = pairs[0] >= pairs[1]
        first = place_of(2 * at + jnp.where(more, 0, 1))
        second = place_of(2 * at + jnp.where(more, 1, 0))
        high, low = jnp.maximum(*pairs), jnp.minimum(*pairs)
        for m in range(1, slots // 2 + 1):
            for n in range(1, m + 1):
                pl.when((high == m) & (low == n))(functools.partial(branch, [first + (m,), second + (n,)]))
        return carry

    lax.fori_loop(0, sources * per // 2, two, 0)
    each = sources // len(out_refs)
    for n, out_ref in enumerate(out_refs):
        for m in range(each):
            out_ref[m * tokens : (m + 1) * tokens, :] = held[n * each + m]


def attend(qkv, place, lists, counts, step, width, each, at_lane=0):
    sources, tokens, _ = qkv.shape
    slots = lists.shape[1] // counts.shape[1]
    return pl.pallas_call(
        functools.partial(attend_kernel, step, at_lane, width, slots),
        out_shape=[jax.ShapeDtypeStruct((each * tokens, width), jnp.bfloat16)] * (sources // each),
        in_specs=[SMEM, SMEM, SMEM, VMEM],
        out_specs=[VMEM] * (sources // each),
        scratch_shapes=[pltpu.VMEM((sources, tokens, width), jnp.bfloat16)],
        compiler_params=limit(12),
        cost_estimate=FREE,
    )(place, lists, counts, qkv)


def project_kernel(terms, n_rows, n_blocks, n_before, *refs):
    rows, blocks = refs[:n_rows], refs[n_rows : n_rows + n_blocks]
    before = refs[n_rows + n_blocks : n_rows + n_blocks + n_before]
    out_refs = refs[n_rows + n_blocks + n_before : -4]
    held, lefts, sem, row_sem = refs[-4:]
    slots = held.shape[0]
    row_copies = []
    for n, (_, picked, cut) in enumerate(terms):
        for k, (r, lane) in enumerate(picked):
            wide = lefts.shape[2] // len(picked)
            source = rows[r].at[pl.ds(cut.start, cut.stop - cut.start), pl.ds(lane, wide)]
            target = lefts.at[n, :, pl.ds(k * wide, wide)]
            row_copies.append(pltpu.make_async_copy(source, target, row_sem.at[n, k]))
    copies = []
    for n, (pieces, _, _) in enumerate(terms):
        at = 0
        copies.append([])
        for k, piece in enumerate(pieces):
            tall = blocks[piece].shape[0]
            target = held.at[n % slots, pl.ds(at, tall), :]
            copies[-1].append(pltpu.make_async_copy(blocks[piece], target, sem.at[n % slots, k]))
            at += tall
    for copy in row_copies + sum(copies[:slots], []):
        copy.start()
    for copy in row_copies:
        copy.wait()
    step = held.shape[-1] // 4
    for n in range(len(terms)):
        for copy in copies[n]:
            copy.wait()
        left = lefts[n]
        for at in range(0, held.shape[-1], step):
            cols = slice(at, at + step)
            part = jnp.dot(left, held[n % slots, :, cols], preferred_element_type=jnp.float32)
            tall = part.shape[0] // len(out_refs)
            for m, out_ref in enumerate(out_refs):
                mine = part[m * tall : (m + 1) * tall]
                if n:
                    mine = mine + out_ref[:, cols]
                elif before:
                    mine = mine + before[m][:, cols]
                out_ref[:, cols] = mine
        if n + slots < len(terms):
            for copy in copies[n + slots]:
                copy.start()


def project(rows, blocks, terms, before, outs):
    cut = terms[0][2]
    tall = cut.stop - cut.start
    wide = blocks[0].shape[1]
    depth = sum(blocks[piece].shape[0] for piece in terms[0][0])
    slots = min(4, len(terms))
    return pl.pallas_call(
        functools.partial(project_kernel, terms, len(rows), len(blocks), len(before)),
        out_shape=[jax.ShapeDtypeStruct((tall // outs, wide), jnp.float32)] * outs,
        in_specs=[ANY] * (len(rows) + len(blocks)) + [VMEM] * len(before),
        out_specs=[VMEM] * outs,
        scratch_shapes=[
            pltpu.VMEM((slots, depth, wide), jnp.bfloat16),
            pltpu.VMEM((len(terms), tall, depth), jnp.bfloat16),
            pltpu.SemaphoreType.DMA((slots, 2)),
            pltpu.SemaphoreType.DMA((len(terms), 2)),
        ],
        compiler_params=limit(36),
        cost_estimate=FREE,
    )(*rows, *blocks, *before)


def along_z(pairs):
    return [(2 * i + c, 2 * j + c) for i, j in pairs for c in (0, 1)]


def after(value, *others):
    return lax.optimization_barrier((value, *others))[0]


def xor(p, groups):
    return [(i, i ^ p) for i in range(groups)]


UP = [(0, 1), (1, 2), (2, 3)]
DOWN = [(j, i) for i, j in UP]


def exchange(x):
    return lax.all_to_all(x, "seq", split_axis=0, concat_axis=0, tiled=True)


def shards_lines(fields, weight, rank, lists, counts, here, width):
    groups = 8
    chip = lax.axis_index("seq") // 2
    place = jnp.stack([lax.axis_index("fsdp"), rank]).astype(jnp.int32)
    n, tokens = weight.shape[0], fields[0].shape[0]

    both = slice(0, 2 * tokens)

    def along(value, axis, pairs):
        return lax.ppermute(value, axis, pairs)

    def send_back(out):
        return [out[0]] + [along(out[p], "seq", xor(2 * p, groups)) for p in (1, 2, 3)]

    def attend_step(qkv, step, at_lane=0):
        return attend(qkv, place, lists, counts, step, width, 2, at_lane)

    def sides(block):
        return [along(block, "fsdp", xor(1, 4)), along(block, "fsdp", xor(2, 4))]

    def fence(*values):
        return lax.optimization_barrier(values)

    (x0,) = lay_out(fields, place, ((0,),), groups, here, width, [])
    qkv0 = exchange(x0)
    up, down = along(weight, "seq", along_z(UP)), along(weight, "seq", along_z(DOWN))
    x1, x2, x3 = lay_out(fields, place, ((1,), (2,), (3,)), groups, here, width, [x0])
    up, down, qkv0, x1, x2, x3 = fence(up, down, qkv0, x1, x2, x3)
    near = jnp.concatenate([weight, jnp.where(chip % 2 == 0, down, up)], axis=0)
    qkv1 = exchange(x1)
    up2, down2 = along(up, "seq", along_z(UP[1:])), along(down, "seq", along_z(DOWN[:2]))
    near_sides = sides(near)
    out0 = attend_step(qkv0, 0)
    up2, down2, qkv1, near_sides, out0 = fence(up2, down2, qkv1, near_sides, out0)
    qkv2 = exchange(after(x2, qkv1))
    last = along(jnp.where(chip == 2, up2, down2), "seq", along_z([(1, 0), (2, 3)]))
    near_corner = [along(near, "fsdp", xor(3, 4))]
    back0 = send_back(out0)
    out1 = attend_step(qkv1, 1)
    last, qkv2, back0, near_corner = fence(last, qkv2, back0, near_corner)
    inner = (chip == 1) | (chip == 2)
    low = chip < 2
    opposite = jnp.where(inner, jnp.where(low, down, up), last)
    far = jnp.concatenate([jnp.where(low, down2, up2), opposite], axis=0)
    qkv3 = exchange(after(x3, qkv2, *out1))
    far_sides = sides(far)
    back1 = send_back(out1)
    out2 = attend_step(qkv2, 2)
    joined = jnp.concatenate(back0, axis=1)
    halves = [far_sides[0][:n], far_sides[1][n:]]
    qkv3, far_sides, halves, back1, out2, joined = fence(qkv3, far_sides, halves, back1, out2, joined)
    joined1 = jnp.concatenate(back1, axis=1)
    back2 = send_back(out2)
    out3 = attend_step(qkv3, 3)
    far_corner = [along(halves[0], "fsdp", xor(2, 4)), along(halves[1], "fsdp", xor(1, 4))]
    back2, out3, joined1 = fence(back2, out3, joined1)
    back3 = send_back(out3)

    sides_all = [near] + near_sides + [far] + far_sides
    rows = [joined, joined1] + back2
    early = [((0,), ((0, 0),), both), ((3,), ((0, 2 * width),), both)]
    early += [((1,), ((1, 0),), both), ((4,), ((1, 2 * width),), both)]
    early += [((2,), ((2, 0), (3, 0)), both), ((5,), ((4, 0), (5, 0)), both)]
    mine, theirs = project(rows, sides_all, early, [], 2)

    def finish(cut, before):
        near_pieces = tuple(range(len(near_corner)))
        far_pieces = tuple(range(len(near_corner), len(near_corner + far_corner)))
        terms = [(near_pieces, ((0, 0), (1, 0)), cut), (far_pieces, ((2, 0), (3, 0)), cut)]
        return project(back3, near_corner + far_corner, terms, [before], 1)[0]

    theirs = finish(slice(tokens, 2 * tokens), theirs)
    given = along(theirs.astype(jnp.bfloat16), "seq", xor(1, groups))
    mine = finish(slice(0, tokens), mine)
    return (mine + given.astype(jnp.float32)).astype(jnp.bfloat16)


def shards_any(fields, weight, rank, lists, counts, here, width, groups):
    place = jnp.stack([0 * rank, rank]).astype(jnp.int32)
    rows = weight.shape[0]
    gathered = lax.all_gather(weight, ("fsdp", "seq"), axis=0, tiled=True)
    gathered = gathered.reshape(here, width // rows, groups, rows, -1).transpose(0, 2, 1, 3, 4)
    gathered = gathered.reshape(here, groups, width, -1)
    ready = lay_out(fields, place, tuple((m,) for m in range(here)), groups, here, width, [])
    result = None
    for member in range(here):
        out = attend(exchange(ready[member]), place, lists, counts, member, width, 1)
        for p in range(groups):
            part = jnp.dot(
                lax.ppermute(out[p], "seq", xor(p, groups)) if p else out[0],
                lax.dynamic_index_in_dim(gathered[member], rank ^ p, 0, keepdims=False),
                preferred_element_type=jnp.float32,
            )
            result = part if result is None else result + part
    return result.astype(jnp.bfloat16)


def shards(queries, keys, values, out_weight, block_lists, block_counts):
    groups = lax.axis_size("seq")
    rank = lax.axis_index("seq")
    head_count = block_counts.shape[1]
    width = queries.shape[2] // head_count
    here = head_count // groups
    lists = lax.dynamic_slice_in_dim(block_lists[0], rank * here, here).reshape(here, -1)
    counts = lax.dynamic_slice_in_dim(block_counts[0], rank * here, here)
    fields = [x[0] for x in (queries, keys, values)]
    if groups == 8 and here == 4 and lax.axis_size("fsdp") == 4 and out_weight.shape[0] == width:
        result = shards_lines(fields, out_weight, rank, lists, counts, here, width)
    else:
        result = shards_any(fields, out_weight, rank, lists, counts, here, width, groups)
    return result[None]


def solution(mesh):
    return jax.shard_map(
        shards,
        mesh=mesh,
        in_specs=(
            P("fsdp", "seq", None),
            P("fsdp", "seq", None),
            P("fsdp", "seq", None),
            P(("seq", "fsdp"), None),
            P("fsdp", None, None, None),
            P("fsdp", None, None),
        ),
        out_specs=P("fsdp", "seq", None),
        check_vma=False,
    )
```
